32 devices in a mesh: groups: 1, col: 16 (over z, y, x), facet: 1, pol: 2 (over core).
Axes of the slice: x: 2, y: 2, z: 4, core: 2. Of those that a mesh axis runs over, the one named last changes fastest.
Arguments:
- facets: float32 [16, 2, 8, 4096], P(('groups', 'col'), 'pol', 'facet'), may hold values from -6 to 6
- facet_offsets: int32 [16], P(('groups', 'col')), may hold values from 0 to 65535
- subgrid_offsets: int32 [16], P('groups'), may hold values from 0 to 65535
- row_counts: int32 [16], P(('groups', 'col', 'facet')), may hold values from 1536 to 2048, as said below
- dest_column: int32 [32768], P(('groups', 'col', 'facet')), may hold values from 0 to 15, as said below
- grid_row: int32 [32768], P(('groups', 'col', 'facet')), may hold values from 0 to 7
- position: float32 [32768], P(('groups', 'col', 'facet')), may hold values from 4 to 123
- observed: float32 [2, 2, 32768], P('pol', None, ('groups', 'col', 'facet')), may hold values from -6 to 6
Outputs:
- column_grid: float32 [16, 2, 8, 256], P(('groups', 'col'), 'pol', 'facet')
- residual: float32 [2, 2, 32768], P('pol', None, ('groups', 'col', 'facet'))
The draws below stay inside these ranges and needn't reach their ends.
Inputs may be any that keep to these rules, and one draw needn't show every extreme that they name: The live rows of each shard are its first row_counts rows; some shard has all 2048 rows live. `dest_column`: among the live rows of one shard no column is named more than 256 times; for each facet index, some column is named exactly 256 times by the live rows of every shard with that facet index.
All inputs are finite; a program needn't handle non-finite values.
Results may differ from the reference program's by a relative error of at most 0.0037.
Values sent between devices are 32-bit elements; how exact they have to be, the bound alone decides.
A program may use at most 64 MiB of HBM per device.

```python
import math
import jax
import jax.numpy as jnp
from jax import lax

NIMG = 65536
YF = 4096
M = 128
POL = 2
S = 8
SLAB_DEV = 8
ROWS_DEV = 2048
COLS = 16
FACET_BLOCKS = 1
SLAB = 8
SHARDS = 16
VROWS = 32768
CAP = 256


def route_tables(key):
    live_counts = jax.random.randint(jax.random.fold_in(key, 11), (SHARDS,), ROWS_DEV * 3 // 4, ROWS_DEV + 1)
    full_shard = jax.random.randint(jax.random.fold_in(key, 12), (), 0, SHARDS)
    live_counts = jnp.where(jnp.arange(SHARDS) == full_shard, ROWS_DEV, live_counts).astype(jnp.int32)
    heavy_cols = jax.random.randint(jax.random.fold_in(key, 13), (FACET_BLOCKS,), 0, COLS).astype(jnp.int32)
    shard_keys = jax.random.split(jax.random.fold_in(key, 14), SHARDS)

    def one_shard(shard_key, shard_id, live_count):
        heavy_col = heavy_cols[shard_id % FACET_BLOCKS]
        others = jax.random.permutation(jax.random.fold_in(shard_key, 1), (COLS - 1) * CAP).astype(jnp.int32)
        other_dest = others // CAP
        other_dest = other_dest + (other_dest >= heavy_col).astype(jnp.int32)
        listed = jnp.concatenate([jnp.full((CAP,), heavy_col, jnp.int32), other_dest])[:ROWS_DEV]
        places = jnp.arange(ROWS_DEV, dtype=jnp.int32)
        shuffled = jax.random.permutation(jax.random.fold_in(shard_key, 2), ROWS_DEV).astype(jnp.int32)
        scores = jnp.where(places < live_count, shuffled, ROWS_DEV + places)
        ordering = jnp.argsort(scores, stable=True)
        return jnp.zeros((ROWS_DEV,), jnp.int32).at[ordering].set(listed)
    destinations = jax.vmap(one_shard)(shard_keys, jnp.arange(SHARDS, dtype=jnp.int32), live_counts)
    return (live_counts, destinations.reshape(-1).astype(jnp.int32))


def draw_row_counts(key, part):
    return route_tables(key)[0]


def draw_dest_column(key, part):
    return route_tables(key)[1]


def touch_ends(drawn, key, smallest, high):
    longest = drawn.shape.index(max(drawn.shape))
    spots = []
    for shift in (0, 1):
        where = [jax.random.randint(jax.random.fold_in(key, axis), (), 0, length) for axis, length in enumerate(drawn.shape)]
        where[longest] = (where[longest] + shift) % drawn.shape[longest]
        spots.append(tuple(where))
    return drawn.at[spots[0]].set(smallest).at[spots[1]].set(high)


def levels(stream_key, dims, cuts, low, largest):
    def one(dim, blocks):
        draws = jax.random.uniform(jax.random.fold_in(jax.random.fold_in(stream_key, 6), dim), (blocks,), jnp.float32, low / len(cuts), largest / len(cuts))
        return jnp.repeat(jnp.exp(draws), dims[dim] // blocks).reshape((-1,) + (1,) * (len(dims) - dim - 1))

    level = one(*cuts[0])
    for cut in cuts[1:]:
        level = level * one(*cut)
    return level


def bell_draw(rng, dims, spread, bound, cuts=(), kind=jnp.bfloat16):
    array = spread * jax.random.normal(rng, dims, jnp.float32)
    if cuts:
        array = array * levels(rng, dims, cuts, -0.22, 0.18)
    return jnp.clip(array, -bound, bound).astype(kind)


def setup_inputs(seed: int = 0, part: int = 0) -> dict:
    arg_keys = jax.random.split(jax.random.key(seed), 9)
    part_splits = jax.random.split(jax.random.fold_in(arg_keys[8], part), 9)
    return {
        "facets": bell_draw(part_splits[0], (COLS, POL, SLAB, YF), 1.0, 6.0, ((0, 16), (1, 2)), jnp.float32),
        "facet_offsets": touch_ends(jax.random.randint(part_splits[1], (COLS,), 0, NIMG), jax.random.fold_in(part_splits[1], 1), 0, NIMG - 1).astype(jnp.int32),
        "subgrid_offsets": touch_ends(jax.random.randint(part_splits[2], (COLS,), 0, NIMG), jax.random.fold_in(part_splits[2], 1), 0, NIMG - 1).astype(jnp.int32),
        "row_counts": draw_row_counts(jax.random.fold_in(jax.random.fold_in(arg_keys[8], part), 71), part),
        "dest_column": draw_dest_column(jax.random.fold_in(jax.random.fold_in(arg_keys[8], part), 71), part),
        "grid_row": touch_ends(jax.random.randint(part_splits[5], (VROWS,), 0, SLAB_DEV), jax.random.fold_in(part_splits[5], 1), 0, SLAB_DEV - 1).astype(jnp.int32),
        "position": jnp.clip(4.0 + 119.0 * jax.random.uniform(part_splits[6], (VROWS,), jnp.float32) ** levels(part_splits[6], (VROWS,), ((0, 16),), -0.2, 0.2), 4.0, 123.0),
        "observed": bell_draw(part_splits[7], (POL, 2, VROWS), 1.0, 6.0, ((0, 2), (2, 16)), jnp.float32),
    }


TWO_PI = 2.0 * math.pi

def product_mod(left_value, right_value, modulus):
    upper_part = left_value // 256 * right_value % modulus
    return (upper_part * 256 + left_value % 256 * right_value) % modulus

def taper_values(pixels):
    places = jnp.arange(pixels, dtype=jnp.int32).astype(jnp.float32)
    offset = (2.0 * places + 1.0) / pixels - 1.0
    squared = 1.0 - offset * offset
    return squared * squared

def phase_table(pixels, frequency_count):
    places = jnp.arange(pixels, dtype=jnp.int32)[:, None]
    frequency = jnp.arange(frequency_count, dtype=jnp.int32)[None, :]
    angles = (places * frequency % NIMG).astype(jnp.float32) * (TWO_PI / NIMG)
    return jnp.concatenate([jnp.cos(angles), -jnp.sin(angles)], axis=1).astype(jnp.bfloat16)

def column_term(facet_rows, window, dft_table, column_offset, facet_offset):
    pixels = facet_rows.shape[1]
    row_total = facet_rows.shape[0]
    frequency_count = dft_table.shape[1] // 2
    places = jnp.arange(pixels, dtype=jnp.int32)
    angles = (places * column_offset % NIMG).astype(jnp.float32) * (TWO_PI / NIMG)
    scaled = facet_rows * window
    modulated = jnp.concatenate([scaled * jnp.cos(angles), -(scaled * jnp.sin(angles))], axis=0).astype(jnp.bfloat16)
    product = jnp.dot(modulated, dft_table, preferred_element_type=jnp.float32)
    real_part = product[:row_total, :frequency_count] - product[row_total:, frequency_count:]
    imag_part = product[:row_total, frequency_count:] + product[row_total:, :frequency_count]
    frequency = jnp.arange(frequency_count, dtype=jnp.int32)
    turn_index = product_mod(facet_offset, (column_offset + frequency) % NIMG, NIMG)
    rotation = turn_index.astype(jnp.float32) * (TWO_PI / NIMG)
    norm_factor = 1.0 / math.sqrt(NIMG)
    cos_turn = jnp.cos(rotation) * norm_factor
    sin_turn = -jnp.sin(rotation) * norm_factor
    return jnp.concatenate([real_part * cos_turn - imag_part * sin_turn, real_part * sin_turn + imag_part * cos_turn], axis=1)

def reference(facets, facet_offsets, subgrid_offsets, row_counts, dest_column, grid_row, position, observed):
    window = taper_values(YF)
    dft_table = phase_table(YF, M)
    rows_all = facets.reshape(COLS, POL * SLAB, YF)

    def one_column(column):
        column_offset = subgrid_offsets[column]

        def add_facet(partial_value, pieces):
            return (partial_value + column_term(pieces[0], window, dft_table, column_offset, pieces[1]), None)
        partial_value, unused = lax.scan(add_facet, jnp.zeros((POL * SLAB, 2 * M), jnp.float32), (rows_all, facet_offsets))
        return partial_value
    column_grid = lax.map(one_column, jnp.arange(COLS, dtype=jnp.int32)).reshape(COLS, POL, SLAB, 2 * M)
    flat_grid = column_grid.reshape(-1)
    row_index = jnp.arange(VROWS, dtype=jnp.int32)
    shard_id = row_index // ROWS_DEV
    live_rows = row_index % ROWS_DEV < row_counts[shard_id]
    target_row = shard_id % FACET_BLOCKS * SLAB_DEV + grid_row
    base_cell = jnp.floor(position).astype(jnp.int32) - S // 2 + 1
    outputs = []
    for polarization in range(POL):
        row_start = ((dest_column * POL + polarization) * SLAB + target_row) * (2 * M)
        real_sum = jnp.zeros((VROWS,), jnp.float32)
        imag_sum = jnp.zeros((VROWS,), jnp.float32)
        for kernel_step in range(S):
            cell_index = base_cell + kernel_step
            distance = cell_index.astype(jnp.float32) - position
            scaled_dist = 2.0 * distance / S
            weight = (1.0 - scaled_dist * scaled_dist) * (1.0 - scaled_dist * scaled_dist)
            real_sum = real_sum + weight * jnp.take(flat_grid, row_start + cell_index)
            imag_sum = imag_sum + weight * jnp.take(flat_grid, row_start + M + cell_index)
        real_out = jnp.where(live_rows, observed[polarization, 0] - real_sum, 0.0)
        imag_out = jnp.where(live_rows, observed[polarization, 1] - imag_sum, 0.0)
        outputs.append(jnp.stack([real_out, imag_out]))
    return (column_grid, jnp.stack(outputs))
```

```python
import functools
import math

import jax
import jax.numpy as jnp
import ml_dtypes
import numpy as np
from jax import lax
from jax.experimental import pallas as pl
from jax.experimental.pallas import tpu as pltpu
from jax.sharding import PartitionSpec as P

NIMG = 65536
M = 128
S = 8
TWO_PI = 2.0 * math.pi
MESH = pl.DeviceIdType.MESH


def dft_constant(pixels):
    places = np.arange(pixels, dtype=np.int64)[:, None]
    frequency = np.arange(M, dtype=np.int64)[None, :]
    angles = (places * frequency % NIMG).astype(np.float64) * (TWO_PI / NIMG)
    table = np.concatenate([np.cos(angles), -np.sin(angles)], axis=1)
    return table.astype(np.float32).astype(ml_dtypes.bfloat16)


def cos_sin(turns):
    quarter = (turns + NIMG // 8) >> 14
    x = (turns - (quarter << 14)).astype(jnp.float32) * (TWO_PI / NIMG)
    z = x * x
    sine = x + x * z * (-1.6666654611e-1 + z * (8.3321608736e-3 - z * 1.9515295891e-4))
    cosine = 1.0 - 0.5 * z + z * z * (
        4.166664568298827e-2 + z * (-1.388731625493765e-3 + z * 2.443315711809948e-5)
    )
    odd = (quarter & 1) == 1
    cos_sign = (1 - ((quarter + 1) & 2)).astype(jnp.float32)
    sin_sign = (1 - (quarter & 2)).astype(jnp.float32)
    return jnp.where(odd, sine, cosine) * cos_sign, jnp.where(odd, cosine, sine) * sin_sign


def kernel(
    n,
    facets,
    facet_offset,
    offsets,
    row_count,
    dest,
    grid_row,
    position,
    observed,
    table_hbm,
    grid_out,
    residual,
    table,
    cos_ref,
    sin_ref,
    modulated,
    turn_cos,
    turn_sin,
    terms,
    arrived,
    grid,
    one_hot,
    weights,
    table_sem,
    send1,
    recv1,
    send2,
    recv2,
):
    me = lax.axis_index("col")
    rows, pixels = facets.shape[2], facets.shape[3]
    peers = [lax.rem(me + d, n) for d in range(n)]

    load = pltpu.make_async_copy(table_hbm, table, table_sem)
    load.start()
    barrier = pltpu.get_barrier_semaphore()
    for d in range(1, n):
        pl.semaphore_signal(barrier, inc=1, device_id={"col": peers[d]}, device_id_type=MESH)

    spot = lax.broadcasted_iota(jnp.int32, (n, 128), 0)
    lane = lax.broadcasted_iota(jnp.int32, (n, 128), 1)
    offset = jnp.zeros((n, 128), jnp.int32)
    for d in range(n):
        offset = jnp.where(spot == d, offsets[peers[d]], offset)
    turn = (facet_offset[0] * ((offset + lane) & (NIMG - 1))) & (NIMG - 1)
    cosine, sine = cos_sin(turn)
    norm_factor = 1.0 / math.sqrt(NIMG)
    turn_cos[...] = cosine * norm_factor
    turn_sin[...] = -sine * norm_factor

    for j in range(pixels // 128):
        cosine, sine = cos_sin(((lane + j * 128) * offset) & (NIMG - 1))
        cos_ref[:, j * 128 : (j + 1) * 128] = cosine
        sin_ref[:, j * 128 : (j + 1) * 128] = -sine

    step = 1024
    for j in range(pixels // step):
        cut = slice(j * step, (j + 1) * step)
        places = (lax.broadcasted_iota(jnp.int32, (rows, step), 1) + j * step).astype(jnp.float32)
        x = (2.0 * places + 1.0) / pixels - 1.0
        squared = 1.0 - x * x
        scaled = facets[0, 0, :, cut] * (squared * squared)
        for d in range(n):
            modulated[2 * rows * d : 2 * rows * (d + 1), cut] = jnp.concatenate(
                [scaled * cos_ref[d : d + 1, cut], scaled * sin_ref[d : d + 1, cut]], axis=0
            ).astype(jnp.bfloat16)

    load.wait()
    product = jnp.dot(modulated[...], table[...], preferred_element_type=jnp.float32)
    for d in range(n):
        upper = product[2 * rows * d : 2 * rows * d + rows]
        lower = product[2 * rows * d + rows : 2 * rows * (d + 1)]
        real_part = upper[:, :M] - lower[:, M:]
        imag_part = upper[:, M:] + lower[:, :M]
        ct, st = turn_cos[d : d + 1, :], turn_sin[d : d + 1, :]
        terms[d, :, :M] = real_part * ct - imag_part * st
        terms[d, :, M:] = real_part * st + imag_part * ct

    pl.semaphore_wait(barrier, n - 1)

    def scatter_copy(d):
        return pltpu.make_async_remote_copy(
            src_ref=terms.at[d],
            dst_ref=arrived.at[d],
            send_sem=send1.at[d],
            recv_sem=recv1.at[d],
            device_id={"col": peers[d]},
            device_id_type=MESH,
        )

    for d in range(1, n):
        scatter_copy(d).start()

    total_rows = n * rows
    for j in range(dest.shape[0]):
        cut = slice(j * 128, (j + 1) * 128)
        wanted = dest[j : j + 1, :] * rows + grid_row[j : j + 1, :]
        hot = (lax.broadcasted_iota(jnp.int32, (total_rows, 128), 0) == wanted).astype(jnp.float32)
        hot = hot.astype(jnp.bfloat16)
        one_hot[:total_rows, cut] = hot
        one_hot[total_rows:, cut] = hot
        cell = lax.broadcasted_iota(jnp.int32, (M, 128), 0).astype(jnp.float32)
        r = (cell - position[j : j + 1, :]) * (2.0 / S)
        tap = jnp.maximum(1.0 - r * r, 0.0)
        weights[:, cut] = tap * tap

    total = terms[0]
    for d in range(1, n):
        scatter_copy(d).wait_recv()
        total = total + arrived[d]
    grid[pl.ds(me, 1)] = total[None]
    grid_out[0, 0] = total

    def gather_copy(d):
        return pltpu.make_async_remote_copy(
            src_ref=grid.at[me],
            dst_ref=grid.at[me],
            send_sem=send2.at[d],
            recv_sem=recv2.at[d],
            device_id={"col": peers[d]},
            device_id_type=MESH,
        )

    for d in range(1, n):
        gather_copy(d).start()
    for d in range(1, n):
        scatter_copy(d).wait_send()
    for d in range(1, n):
        gather_copy(d).wait_recv()

    turned = grid[...].reshape(total_rows, 2 * M).T
    high = turned.astype(jnp.bfloat16)
    low = (turned - high.astype(jnp.float32)).astype(jnp.bfloat16)
    left = jnp.concatenate([high, low], axis=1)
    live_count = row_count[0]
    step = 256
    for j in range(residual.shape[2] // step):
        cut = slice(j * step, (j + 1) * step)
        picked = jnp.dot(left, one_hot[:, cut], preferred_element_type=jnp.float32)
        w = weights[:, cut]
        real_sum = jnp.sum(picked[:M] * w, axis=0, keepdims=True)
        imag_sum = jnp.sum(picked[M:] * w, axis=0, keepdims=True)
        live = lax.broadcasted_iota(jnp.int32, (1, step), 1) + j * step < live_count
        residual[0, 0:1, cut] = jnp.where(live, observed[0, 0:1, cut] - real_sum, 0.0)
        residual[0, 1:2, cut] = jnp.where(live, observed[0, 1:2, cut] - imag_sum, 0.0)

    for d in range(1, n):
        gather_copy(d).wait_send()


def body(
    facets, facet_offsets, subgrid_offsets, row_counts, dest_column, grid_row, position, observed
):
    n = lax.axis_size("col")
    rows, pixels = facets.shape[2], facets.shape[3]
    count = dest_column.shape[0]
    tall = (count // 128, 128)
    vmem = pl.BlockSpec(memory_space=pltpu.VMEM)
    smem = pl.BlockSpec(memory_space=pltpu.SMEM)
    f32, bf16 = jnp.float32, jnp.bfloat16
    return pl.pallas_call(
        functools.partial(kernel, n),
        out_shape=(
            jax.ShapeDtypeStruct((1, 1, rows, 2 * M), f32),
            jax.ShapeDtypeStruct(observed.shape, f32),
        ),
        in_specs=[vmem, smem, smem, smem, vmem, vmem, vmem, vmem, pl.BlockSpec(memory_space=pl.ANY)],
        out_specs=(vmem, vmem),
        scratch_shapes=[
            pltpu.VMEM((pixels, 2 * M), bf16),
            pltpu.VMEM((n, pixels), f32),
            pltpu.VMEM((n, pixels), f32),
            pltpu.VMEM((2 * rows * n, pixels), bf16),
            pltpu.VMEM((n, M), f32),
            pltpu.VMEM((n, M), f32),
            pltpu.VMEM((n, rows, 2 * M), f32),
            pltpu.VMEM((n, rows, 2 * M), f32),
            pltpu.VMEM((n, rows, 2 * M), f32),
            pltpu.VMEM((2 * n * rows, count), bf16),
            pltpu.VMEM((M, count), f32),
            pltpu.SemaphoreType.DMA,
            pltpu.SemaphoreType.DMA((n,)),
            pltpu.SemaphoreType.DMA((n,)),
            pltpu.SemaphoreType.DMA((n,)),
            pltpu.SemaphoreType.DMA((n,)),
        ],
        compiler_params=pltpu.CompilerParams(
            collective_id=0, has_side_effects=True, vmem_limit_bytes=48 * 1024 * 1024
        ),
    )(
        facets,
        facet_offsets,
        subgrid_offsets,
        row_counts,
        dest_column.reshape(tall),
        grid_row.reshape(tall),
        position.reshape(tall),
        observed,
        jnp.asarray(dft_constant(pixels)),
    )


def solution(mesh):
    placed = (
        P(("groups", "col"), "pol", "facet", None),
        P(("groups", "col")),
        P("groups"),
        P(("groups", "col", "facet")),
        P(("groups", "col", "facet")),
        P(("groups", "col", "facet")),
        P(("groups", "col", "facet")),
        P("pol", None, ("groups", "col", "facet")),
    )
    return jax.shard_map(
        body,
        mesh=mesh,
        in_specs=placed,
        out_specs=(
            P(("groups", "col"), "pol", "facet", None),
            P("pol", None, ("groups", "col", "facet")),
        ),
        check_vma=False,
    )
```

```python
import functools
import math

import jax
import jax.numpy as jnp
import ml_dtypes
import numpy as np
from jax import lax
from jax.experimental import pallas as pl
from jax.experimental.pallas import tpu as pltpu
from jax.sharding import PartitionSpec as P

NIMG = 65536
M = 128
S = 8
NEAR = 4
TWO_PI = 2.0 * math.pi
MESH = pl.DeviceIdType.MESH


def dft_constant(pixels):
    places = np.arange(pixels, dtype=np.int64)[:, None]
    frequency = np.arange(M, dtype=np.int64)[None, :]
    angles = (places * frequency % NIMG).astype(np.float64) * (TWO_PI / NIMG)
    table = np.concatenate([np.cos(angles), -np.sin(angles)], axis=1)
    return table.astype(np.float32).astype(ml_dtypes.bfloat16)


def cos_sin(turns):
    quarter = (turns + NIMG // 8) >> 14
    x = (turns - (quarter << 14)).astype(jnp.float32) * (TWO_PI / NIMG)
    z = x * x
    sine = x + x * z * (-1.6666654611e-1 + z * (8.3321608736e-3 - z * 1.9515295891e-4))
    cosine = 1.0 - 0.5 * z + z * z * (
        4.166664568298827e-2 + z * (-1.388731625493765e-3 + z * 2.443315711809948e-5)
    )
    odd = (quarter & 1) == 1
    cos_sign = (1 - ((quarter + 1) & 2)).astype(jnp.float32)
    sin_sign = (1 - (quarter & 2)).astype(jnp.float32)
    return jnp.where(odd, sine, cosine) * cos_sign, jnp.where(odd, cosine, sine) * sin_sign


def kernel(
    n,
    *refs,
):
    sources, (grid_out, residual_out), local, rest = refs[:9], refs[9:11], refs[11:20], refs[20:]
    facet_offset, offsets, row_count, facets, dest, grid_row, position, observed, table = local
    cos_ref, sin_ref, modulated, turn_cos, turn_sin, terms, arrived, grid, one_hot, weights = rest[:10]
    arrived_far, partial, residual = rest[10:13]
    load_sem, store_sem, send1, recv1, send2, recv2, send3, recv3 = rest[13:]
    me = lax.axis_index("col")
    rows, pixels = facets.shape[2], facets.shape[3]
    near = NEAR
    far = n // near
    high, low = me // near, lax.rem(me, near)
    near_peers = [high * near + lax.rem(low + d, near) for d in range(near)]
    far_peers = [lax.rem(high + e, far) * near + low for e in range(far)]
    columns = [near * h + lax.rem(low + d, near) for d in range(near) for h in range(far)]

    loads = [
        pltpu.make_async_copy(source, target, load_sem.at[i])
        for i, (source, target) in enumerate(zip(sources, local))
    ]
    for load in loads:
        load.start()
    barrier = pltpu.get_barrier_semaphore()
    for peer in near_peers[1:] + far_peers[1:]:
        pl.semaphore_signal(barrier, inc=1, device_id={"col": peer}, device_id_type=MESH)

    loads[0].wait()
    loads[1].wait()
    spot = lax.broadcasted_iota(jnp.int32, (n, 128), 0)
    lane = lax.broadcasted_iota(jnp.int32, (n, 128), 1)
    offset = jnp.zeros((n, 128), jnp.int32)
    for d in range(n):
        offset = jnp.where(spot == d, offsets[columns[d]], offset)
    turn = (facet_offset[0] * ((offset + lane) & (NIMG - 1))) & (NIMG - 1)
    cosine, sine = cos_sin(turn)
    norm_factor = 1.0 / math.sqrt(NIMG)
    turn_cos[...] = cosine * norm_factor
    turn_sin[...] = -sine * norm_factor

    for j in range(pixels // 128):
        cosine, sine = cos_sin(((lane + j * 128) * offset) & (NIMG - 1))
        cos_ref[:, j * 128 : (j + 1) * 128] = cosine
        sin_ref[:, j * 128 : (j + 1) * 128] = -sine

    loads[3].wait()
    step = 1024
    for j in range(pixels // step):
        cut = slice(j * step, (j + 1) * step)
        places = (lax.broadcasted_iota(jnp.int32, (rows, step), 1) + j * step).astype(jnp.float32)
        x = (2.0 * places + 1.0) / pixels - 1.0
        squared = 1.0 - x * x
        scaled = facets[0, 0, :, cut] * (squared * squared)
        for d in range(n):
            modulated[2 * rows * d : 2 * rows * (d + 1), cut] = jnp.concatenate(
                [scaled * cos_ref[d : d + 1, cut], scaled * sin_ref[d : d + 1, cut]], axis=0
            ).astype(jnp.bfloat16)

    loads[8].wait()
    product = jnp.dot(modulated[...], table[...], preferred_element_type=jnp.float32)
    for d in range(n):
        upper = product[2 * rows * d : 2 * rows * d + rows]
        lower = product[2 * rows * d + rows : 2 * rows * (d + 1)]
        real_part = upper[:, :M] - lower[:, M:]
        imag_part = upper[:, M:] + lower[:, :M]
        ct, st = turn_cos[d : d + 1, :], turn_sin[d : d + 1, :]
        terms[d // far, d % far, :, :M] = real_part * ct - imag_part * st
        terms[d // far, d % far, :, M:] = real_part * st + imag_part * ct

    pl.semaphore_wait(barrier, near + far - 2)

    def send(source, target, send_sem, recv_sem, peer):
        return pltpu.make_async_remote_copy(
            src_ref=source,
            dst_ref=target,
            send_sem=send_sem,
            recv_sem=recv_sem,
            device_id={"col": peer},
            device_id_type=MESH,
        )

    def first_copy(d, h):
        return send(terms.at[d, h], arrived.at[d, h], send1.at[d, h], recv1.at[d, h], near_peers[d])

    def second_copy(e, h):
        return send(
            partial.at[h], arrived_far.at[e, h], send2.at[e, h], recv2.at[e, h], far_peers[e]
        )

    def third_copy(d, h):
        here = grid.at[near * h + low]
        return send(here, here, send3.at[d, h], recv3.at[d, h], near_peers[d])

    for h in range(far):
        for d in range(1, near):
            first_copy(d, h).start()

    for load in loads[4:8]:
        load.wait()
    loads[2].wait()
    total_rows = n * rows
    for j in range(dest.shape[0]):
        cut = slice(j * 128, (j + 1) * 128)
        wanted = dest[j : j + 1, :] * rows + grid_row[j : j + 1, :]
        hot = (lax.broadcasted_iota(jnp.int32, (total_rows, 128), 0) == wanted).astype(jnp.float32)
        hot = hot.astype(jnp.bfloat16)
        one_hot[:total_rows, cut] = hot
        one_hot[total_rows:, cut] = hot
        cell = lax.broadcasted_iota(jnp.int32, (M, 128), 0).astype(jnp.float32)
        r = (cell - position[j : j + 1, :]) * (2.0 / S)
        tap = jnp.maximum(1.0 - r * r, 0.0)
        weights[:, cut] = tap * tap

    for h in range(far):
        total = terms[0, h]
        for d in range(1, near):
            first_copy(d, h).wait_recv()
            total = total + arrived[d, h]
        partial[h] = total
        for e in range(1, far):
            second_copy(e, h).start()
    for h in range(far):
        total = partial[h]
        for e in range(1, far):
            second_copy(e, h).wait_recv()
            total = total + arrived_far[e, h]
        grid[pl.ds(near * h + low, 1)] = total[None]
        for d in range(1, near):
            third_copy(d, h).start()
    stores = [pltpu.make_async_copy(grid.at[me], grid_out.at[0, 0], store_sem.at[0])]
    stores[0].start()
    for h in range(far):
        for d in range(1, near):
            first_copy(d, h).wait_send()
        for e in range(1, far):
            second_copy(e, h).wait_send()
    for h in range(far):
        for d in range(1, near):
            third_copy(d, h).wait_recv()

    turned = grid[...].reshape(total_rows, 2 * M).T
    coarse = turned.astype(jnp.bfloat16)
    fine = (turned - coarse.astype(jnp.float32)).astype(jnp.bfloat16)
    left = jnp.concatenate([coarse, fine], axis=1)
    live_count = row_count[0]
    step = 256
    for j in range(residual.shape[2] // step):
        cut = slice(j * step, (j + 1) * step)
        picked = jnp.dot(left, one_hot[:, cut], preferred_element_type=jnp.float32)
        w = weights[:, cut]
        real_sum = jnp.sum(picked[:M] * w, axis=0, keepdims=True)
        imag_sum = jnp.sum(picked[M:] * w, axis=0, keepdims=True)
        live = lax.broadcasted_iota(jnp.int32, (1, step), 1) + j * step < live_count
        residual[0, 0:1, cut] = jnp.where(live, observed[0, 0:1, cut] - real_sum, 0.0)
        residual[0, 1:2, cut] = jnp.where(live, observed[0, 1:2, cut] - imag_sum, 0.0)

    stores.append(pltpu.make_async_copy(residual, residual_out, store_sem.at[1]))
    stores[1].start()
    for h in range(far):
        for d in range(1, near):
            third_copy(d, h).wait_send()
    for store in stores:
        store.wait()


def body(
    facets, facet_offsets, subgrid_offsets, row_counts, dest_column, grid_row, position, observed
):
    n = lax.axis_size("col")
    far = n // NEAR
    rows, pixels = facets.shape[2], facets.shape[3]
    count = dest_column.shape[0]
    tall = (count // 128, 128)
    hbm = pl.BlockSpec(memory_space=pltpu.HBM)
    f32, bf16 = jnp.float32, jnp.bfloat16
    arrays = (
        facet_offsets,
        subgrid_offsets,
        row_counts,
        facets,
        dest_column.reshape(tall),
        grid_row.reshape(tall),
        position.reshape(tall),
        observed,
        jnp.asarray(dft_constant(pixels)),
    )
    spaces = [pltpu.SMEM] * 3 + [pltpu.VMEM] * 6
    shapes = (
        jax.ShapeDtypeStruct((1, 1, rows, 2 * M), f32),
        jax.ShapeDtypeStruct(observed.shape, f32),
    )
    return pl.pallas_call(
        functools.partial(kernel, n),
        out_shape=shapes,
        in_specs=[hbm] * len(arrays),
        out_specs=(hbm, hbm),
        scratch_shapes=[
            *[space(array.shape, array.dtype) for space, array in zip(spaces, arrays)],
            pltpu.VMEM((n, pixels), f32),
            pltpu.VMEM((n, pixels), f32),
            pltpu.VMEM((2 * rows * n, pixels), bf16),
            pltpu.VMEM((n, M), f32),
            pltpu.VMEM((n, M), f32),
            pltpu.VMEM((NEAR, far, rows, 2 * M), f32),
            pltpu.VMEM((NEAR, far, rows, 2 * M), f32),
            pltpu.VMEM((n, rows, 2 * M), f32),
            pltpu.VMEM((2 * n * rows, count), bf16),
            pltpu.VMEM((M, count), f32),
            pltpu.VMEM((far, far, rows, 2 * M), f32),
            pltpu.VMEM((far, rows, 2 * M), f32),
            pltpu.VMEM(observed.shape, f32),
            pltpu.SemaphoreType.DMA((len(arrays),)),
            pltpu.SemaphoreType.DMA((2,)),
            pltpu.SemaphoreType.DMA((NEAR, far)),
            pltpu.SemaphoreType.DMA((NEAR, far)),
            pltpu.SemaphoreType.DMA((far, far)),
            pltpu.SemaphoreType.DMA((far, far)),
            pltpu.SemaphoreType.DMA((NEAR, far)),
            pltpu.SemaphoreType.DMA((NEAR, far)),
        ],
        compiler_params=pltpu.CompilerParams(
            collective_id=0, has_side_effects=True, vmem_limit_bytes=64 * 1024 * 1024
        ),
    )(*arrays)


def solution(mesh):
    placed = (
        P(("groups", "col"), "pol", "facet", None),
        P(("groups", "col")),
        P("groups"),
        P(("groups", "col", "facet")),
        P(("groups", "col", "facet")),
        P(("groups", "col", "facet")),
        P(("groups", "col", "facet")),
        P("pol", None, ("groups", "col", "facet")),
    )
    return jax.shard_map(
        body,
        mesh=mesh,
        in_specs=placed,
        out_specs=(
            P(("groups", "col"), "pol", "facet", None),
            P("pol", None, ("groups", "col", "facet")),
        ),
        check_vma=False,
    )
```

```python
import functools
import math

import jax
import jax.numpy as jnp
import ml_dtypes
import numpy as np
from jax import lax
from jax.experimental import pallas as pl
from jax.experimental.pallas import tpu as pltpu
from jax.sharding import PartitionSpec as P

NIMG = 65536
M = 128
S = 8
NEAR = 4
TWO_PI = 2.0 * math.pi
MESH = pl.DeviceIdType.MESH


def dft_constant(pixels):
    places = np.arange(pixels, dtype=np.int64)[:, None]
    frequency = np.arange(M, dtype=np.int64)[None, :]
    angles = (places * frequency % NIMG).astype(np.float64) * (TWO_PI / NIMG)
    table = np.concatenate([np.cos(angles), -np.sin(angles)], axis=1)
    return table.astype(np.float32).astype(ml_dtypes.bfloat16)


def cos_sin(turns):
    quarter = (turns + NIMG // 8) >> 14
    x = (turns - (quarter << 14)).astype(jnp.float32) * (TWO_PI / NIMG)
    z = x * x
    sine = x + x * z * (-1.6666654611e-1 + z * (8.3321608736e-3 - z * 1.9515295891e-4))
    cosine = 1.0 - 0.5 * z + z * z * (
        4.166664568298827e-2 + z * (-1.388731625493765e-3 + z * 2.443315711809948e-5)
    )
    odd = (quarter & 1) == 1
    cos_sign = (1 - ((quarter + 1) & 2)).astype(jnp.float32)
    sin_sign = (1 - (quarter & 2)).astype(jnp.float32)
    return jnp.where(odd, sine, cosine) * cos_sign, jnp.where(odd, cosine, sine) * sin_sign


def kernel(
    n,
    *refs,
):
    sources, (grid_out, residual), local, rest = refs[:9], refs[9:11], refs[11:18], refs[18:]
    facet_offset, row_count = sources[:2]
    offsets, facets, dest, grid_row, position, observed, table = local
    cos_ref, sin_ref, modulated, turn_cos, turn_sin, terms, arrived, grid, one_hot, weights = rest[:10]
    arrived_far, partial = rest[10:12]
    load_sem, send1, recv1, send2, recv2, send3, recv3 = rest[12:]
    me = lax.axis_index("col")
    rows, pixels = facets.shape[2], facets.shape[3]
    near = NEAR
    far = n // near
    high, low = me // near, lax.rem(me, near)
    near_peers = [high * near + lax.rem(low + d, near) for d in range(near)]
    far_peers = [lax.rem(high + e, far) * near + low for e in range(far)]
    columns = [near * h + lax.rem(low + d, near) for d in range(near) for h in range(far)]

    loads = [
        pltpu.make_async_copy(source, target, load_sem.at[i])
        for i, (source, target) in enumerate(zip(sources[2:], local))
    ]
    for load in loads:
        load.start()
    barrier = pltpu.get_barrier_semaphore()
    for peer in near_peers[1:] + far_peers[1:]:
        pl.semaphore_signal(barrier, inc=1, device_id={"col": peer}, device_id_type=MESH)

    loads[0].wait()
    spot = lax.broadcasted_iota(jnp.int32, (n, 128), 0)
    lane = lax.broadcasted_iota(jnp.int32, (n, 128), 1)
    offset = jnp.zeros((n, 128), jnp.int32)
    for d in range(n):
        offset = jnp.where(spot == d, offsets[columns[d]], offset)
    turn = (facet_offset[0] * ((offset + lane) & (NIMG - 1))) & (NIMG - 1)
    cosine, sine = cos_sin(turn)
    norm_factor = 1.0 / math.sqrt(NIMG)
    turn_cos[...] = cosine * norm_factor
    turn_sin[...] = -sine * norm_factor

    for j in range(pixels // 128):
        cosine, sine = cos_sin(((lane + j * 128) * offset) & (NIMG - 1))
        cos_ref[:, j * 128 : (j + 1) * 128] = cosine
        sin_ref[:, j * 128 : (j + 1) * 128] = -sine

    loads[1].wait()
    step = 1024
    for j in range(pixels // step):
        cut = slice(j * step, (j + 1) * step)
        places = (lax.broadcasted_iota(jnp.int32, (rows, step), 1) + j * step).astype(jnp.float32)
        x = (2.0 * places + 1.0) / pixels - 1.0
        squared = 1.0 - x * x
        scaled = facets[0, 0, :, cut] * (squared * squared)
        for d in range(n):
            modulated[2 * rows * d : 2 * rows * (d + 1), cut] = jnp.concatenate(
                [scaled * cos_ref[d : d + 1, cut], scaled * sin_ref[d : d + 1, cut]], axis=0
            ).astype(jnp.bfloat16)

    loads[6].wait()
    product = jnp.dot(modulated[...], table[...], preferred_element_type=jnp.float32)
    for d in range(n):
        upper = product[2 * rows * d : 2 * rows * d + rows]
        lower = product[2 * rows * d + rows : 2 * rows * (d + 1)]
        real_part = upper[:, :M] - lower[:, M:]
        imag_part = upper[:, M:] + lower[:, :M]
        ct, st = turn_cos[d : d + 1, :], turn_sin[d : d + 1, :]
        terms[d // far, d % far, :, :M] = real_part * ct - imag_part * st
        terms[d // far, d % far, :, M:] = real_part * st + imag_part * ct

    pl.semaphore_wait(barrier, near + far - 2)

    def send(source, target, send_sem, recv_sem, peer):
        return pltpu.make_async_remote_copy(
            src_ref=source,
            dst_ref=target,
            send_sem=send_sem,
            recv_sem=recv_sem,
            device_id={"col": peer},
            device_id_type=MESH,
        )

    def first_copy(d):
        return send(terms.at[d], arrived.at[d], send1.at[d], recv1.at[d], near_peers[d])

    def second_copy(e):
        return send(partial, arrived_far.at[e], send2.at[e], recv2.at[e], far_peers[e])

    def third_copy(d):
        return send(grid.at[low], grid.at[low], send3.at[d], recv3.at[d], near_peers[d])

    for d in range(1, near):
        first_copy(d).start()

    for load in loads[2:6]:
        load.wait()
    total_rows = n * rows
    for j in range(dest.shape[0]):
        cut = slice(j * 128, (j + 1) * 128)
        column = dest[j : j + 1, :]
        column = column % near * far + column // near
        wanted = column * rows + grid_row[j : j + 1, :]
        hot = (lax.broadcasted_iota(jnp.int32, (total_rows, 128), 0) == wanted).astype(jnp.float32)
        hot = hot.astype(jnp.bfloat16)
        one_hot[:total_rows, cut] = hot
        one_hot[total_rows:, cut] = hot
        cell = lax.broadcasted_iota(jnp.int32, (M, 128), 0).astype(jnp.float32)
        r = (cell - position[j : j + 1, :]) * (2.0 / S)
        tap = jnp.maximum(1.0 - r * r, 0.0)
        weights[:, cut] = tap * tap

    total = terms[0]
    for d in range(1, near):
        first_copy(d).wait_recv()
        total = total + arrived[d]
    partial[...] = total
    for e in range(1, far):
        second_copy(e).start()
    for e in range(1, far):
        second_copy(e).wait_recv()
        total = total + arrived_far[e]
    grid[pl.ds(low, 1)] = total[None]
    for d in range(1, near):
        third_copy(d).start()
    grid_out[0, 0] = grid[low, high]
    for d in range(1, near):
        first_copy(d).wait_send()
    for e in range(1, far):
        second_copy(e).wait_send()
    for d in range(1, near):
        third_copy(d).wait_recv()

    turned = grid[...].reshape(total_rows, 2 * M).T
    coarse = turned.astype(jnp.bfloat16)
    fine = (turned - coarse.astype(jnp.float32)).astype(jnp.bfloat16)
    left = jnp.concatenate([coarse, fine], axis=1)
    live_count = row_count[0]
    step = 256
    for j in range(residual.shape[2] // step):
        cut = slice(j * step, (j + 1) * step)
        picked = jnp.dot(left, one_hot[:, cut], preferred_element_type=jnp.float32)
        w = weights[:, cut]
        real_sum = jnp.sum(picked[:M] * w, axis=0, keepdims=True)
        imag_sum = jnp.sum(picked[M:] * w, axis=0, keepdims=True)
        live = lax.broadcasted_iota(jnp.int32, (1, step), 1) + j * step < live_count
        residual[0, 0:1, cut] = jnp.where(live, observed[0, 0:1, cut] - real_sum, 0.0)
        residual[0, 1:2, cut] = jnp.where(live, observed[0, 1:2, cut] - imag_sum, 0.0)

    for d in range(1, near):
        third_copy(d).wait_send()


def body(
    facets, facet_offsets, subgrid_offsets, row_counts, dest_column, grid_row, position, observed
):
    n = lax.axis_size("col")
    far = n // NEAR
    rows, pixels = facets.shape[2], facets.shape[3]
    count = dest_column.shape[0]
    tall = (count // 128, 128)
    vmem = pl.BlockSpec(memory_space=pltpu.VMEM)
    smem = pl.BlockSpec(memory_space=pltpu.SMEM)
    hbm = pl.BlockSpec(memory_space=pltpu.HBM)
    f32, bf16 = jnp.float32, jnp.bfloat16
    arrays = (
        facet_offsets,
        row_counts,
        subgrid_offsets,
        facets,
        dest_column.reshape(tall),
        grid_row.reshape(tall),
        position.reshape(tall),
        observed,
        jnp.asarray(dft_constant(pixels)),
    )
    spaces = [pltpu.SMEM] + [pltpu.VMEM] * 6
    shapes = (
        (1, 1, rows, 2 * M),
        observed.shape,
    )
    return pl.pallas_call(
        functools.partial(kernel, n),
        out_shape=tuple(pltpu.VMEM(shape, f32) for shape in shapes),
        in_specs=[smem if array.size == 1 else hbm for array in arrays],
        out_specs=(vmem, vmem),
        scratch_shapes=[
            *[space(array.shape, array.dtype) for space, array in zip(spaces, arrays[2:])],
            pltpu.VMEM((n, pixels), f32),
            pltpu.VMEM((n, pixels), f32),
            pltpu.VMEM((2 * rows * n, pixels), bf16),
            pltpu.VMEM((n, M), f32),
            pltpu.VMEM((n, M), f32),
            pltpu.VMEM((NEAR, far, rows, 2 * M), f32),
            pltpu.VMEM((NEAR, far, rows, 2 * M), f32),
            pltpu.VMEM((NEAR, far, rows, 2 * M), f32),
            pltpu.VMEM((2 * n * rows, count), bf16),
            pltpu.VMEM((M, count), f32),
            pltpu.VMEM((far, far, rows, 2 * M), f32),
            pltpu.VMEM((far, rows, 2 * M), f32),
            pltpu.SemaphoreType.DMA((len(spaces),)),
            pltpu.SemaphoreType.DMA((NEAR,)),
            pltpu.SemaphoreType.DMA((NEAR,)),
            pltpu.SemaphoreType.DMA((far,)),
            pltpu.SemaphoreType.DMA((far,)),
            pltpu.SemaphoreType.DMA((NEAR,)),
            pltpu.SemaphoreType.DMA((NEAR,)),
        ],
        compiler_params=pltpu.CompilerParams(
            collective_id=0, has_side_effects=True, vmem_limit_bytes=40 * 1024 * 1024
        ),
    )(*[
        array if array.size == 1 else pltpu.with_memory_space_constraint(array, pltpu.HBM)
        for array in arrays
    ])


def solution(mesh):
    placed = (
        P(("groups", "col"), "pol", "facet", None),
        P(("groups", "col")),
        P("groups"),
        P(("groups", "col", "facet")),
        P(("groups", "col", "facet")),
        P(("groups", "col", "facet")),
        P(("groups", "col", "facet")),
        P("pol", None, ("groups", "col", "facet")),
    )
    return jax.shard_map(
        body,
        mesh=mesh,
        in_specs=placed,
        out_specs=(
            P(("groups", "col"), "pol", "facet", None),
            P("pol", None, ("groups", "col", "facet")),
        ),
        check_vma=False,
    )
```
